1024 devices in a mesh: fsdp: 64 (over z, core), tensor: 16 (over y, x).
Axes of the slice: x: 4, y: 4, z: 32, core: 2. Of those that a mesh axis runs over, the one named last changes fastest.
Arguments:
- grads: bfloat16 [8192, 16384], P('fsdp', 'tensor'), may hold values from -6 to 6
- assignment: int32 [512], replicated, may hold values from 0 to 703, as said below
- left_root: bfloat16 [704, 512, 512], P('fsdp'), as said below
- right_root: bfloat16 [704, 512, 512], P('fsdp', 'tensor'), as said below
Outputs:
- left_stat: float32 [704, 512, 512], P('fsdp', 'tensor')
- right_stat: float32 [704, 512, 512], P('fsdp', 'tensor')
- preconditioned: bfloat16 [8192, 16384], P('fsdp', 'tensor')
The draws below stay inside these ranges and needn't reach their ends.
Inputs may be any that keep to these rules, and one draw needn't show every extreme that they name: `assignment`: entries are distinct; slot q belongs to owner q // 11; an owner holds at most 11 blocks and at most 2 blocks of one row slab (blocks with the same r). `left_root`: Symmetric. `right_root`: Symmetric.
All inputs are finite; a program needn't handle non-finite values.
Results may differ from the reference program's by a relative error of at most 0.0049.
Values may be sent and summed in bfloat16 or wider, within the bound.
No kernel may reach another device: no remote copies, remote signals or barrier semaphores. Data moves between devices by JAX's collectives and lax.ppermute only.
A program may use at most 64 MiB of HBM per device.

```python
import jax
import jax.numpy as jnp
from jax import lax

BLOCK = 512
ROW_DEV = 128
COL_DEV = 1024
ROWS = 8192
COLS = 16384
SLOTS = 11
SLOT_ALL = 704
N_FSDP = 64
N_TENSOR = 16


def assemble_root(noise_field, diagonal):
    symmetric = (noise_field + jnp.swapaxes(noise_field, 1, 2)) * (0.4 * BLOCK ** (-0.5))
    identity = jnp.eye(BLOCK, dtype=jnp.float32)
    return (symmetric * (1.0 - identity) + identity * diagonal[:, :, None]).astype(jnp.bfloat16)


def draw_assignment(key, part):
    key = jax.random.fold_in(key, 11)
    key_high, key_order, key_rows, key_cols = jax.random.split(key, 4)
    span = BLOCK // ROW_DEV
    row_slabs = N_FSDP // span
    col_blocks = COL_DEV // BLOCK * N_TENSOR
    total = row_slabs * col_blocks
    mean_load = total // N_FSDP
    high_flag = jax.random.permutation(key_high, N_FSDP) < N_FSDP // 2
    loads = jnp.where(high_flag, SLOTS, 2 * mean_load - SLOTS).astype(jnp.int32)
    order = jax.random.permutation(key_order, N_FSDP).astype(jnp.int32)
    ordered_loads = loads[order]
    ends = jnp.cumsum(ordered_loads).astype(jnp.int32)
    starts = ends - ordered_loads
    position = jnp.arange(total, dtype=jnp.int32)
    which = jnp.sum((ends[None, :] <= position[:, None]).astype(jnp.int32), axis=1)
    offset = position - starts[which]
    slot = order[which] * SLOTS + offset
    cycle = 2 * row_slabs
    pair_index = position // cycle
    within = position % cycle
    row_perm = jax.random.permutation(key_rows, row_slabs).astype(jnp.int32)
    col_perm = jax.random.permutation(key_cols, col_blocks).astype(jnp.int32)
    slab = row_perm[within // 2]
    column = col_perm[2 * pair_index + within % 2]
    block_id = slab * col_blocks + column
    return jnp.zeros((total,), jnp.int32).at[block_id].set(slot.astype(jnp.int32))


def draw_left_root(key, part):
    key = jax.random.fold_in(key, 23)
    key_noise, key_diag = jax.random.split(key)
    shape_all = (SLOT_ALL, BLOCK, BLOCK)
    noise_field = jax.random.normal(key_noise, shape_all, jnp.float32)
    diagonal = jnp.exp(jax.random.uniform(key_diag, (SLOT_ALL, BLOCK), jnp.float32, -0.6931472, 0.6931472))
    return assemble_root(noise_field, diagonal)


def draw_right_root(key, part):
    key = jax.random.fold_in(key, 37)
    key_noise, key_diag = jax.random.split(key)
    shape_all = (SLOT_ALL, BLOCK, BLOCK)
    noise_field = jax.random.normal(key_noise, shape_all, jnp.float32)
    diagonal = jnp.exp(jax.random.uniform(key_diag, (SLOT_ALL, BLOCK), jnp.float32, -0.6931472, 0.6931472))
    return assemble_root(noise_field, diagonal)


def block_scale(stream_key, shape, cuts, smallest, high):
    loudness = 1.0
    for axis_at, blocks in cuts:
        draws = jax.random.uniform(jax.random.fold_in(jax.random.fold_in(stream_key, 6), axis_at), (blocks,), jnp.float32, smallest / len(cuts), high / len(cuts))
        loudness = loudness * jnp.repeat(jnp.exp(draws), shape[axis_at] // blocks).reshape((-1,) + (1,) * (len(shape) - 1 - axis_at))
    return loudness


def scatter_about(stream_key, extent, scale, bound, pieces=(), kind=jnp.bfloat16):
    level = block_scale(stream_key, extent, pieces, -0.22, 0.18) if pieces else 1.0
    array = jax.random.normal(stream_key, extent, jnp.float32) * scale * level
    return jnp.minimum(jnp.maximum(array, -bound), bound).astype(kind)


def setup_inputs(seed: int = 0) -> dict:
    key_of = jax.random.split(jax.random.key(seed), 5)
    return {
        "grads": scatter_about(key_of[0], (ROWS, COLS), 1.0, 6.0, ((0, 64), (1, 16))),
        "assignment": draw_assignment(jax.random.fold_in(key_of[4], 71), 0),
        "left_root": draw_left_root(jax.random.fold_in(key_of[4], 71), 0),
        "right_root": draw_right_root(jax.random.fold_in(key_of[4], 71), 0),
    }


def reference(grads, assignment, left_root, right_root):
    row_slabs = ROWS // BLOCK
    col_blocks = COLS // BLOCK
    inverse = 1.0 / BLOCK
    blocks = grads.reshape(row_slabs, BLOCK, col_blocks, BLOCK).transpose(0, 2, 1, 3).reshape(row_slabs * col_blocks, BLOCK, BLOCK)

    def one_block(item_pair):
        gradient, slot_id = item_pair
        left_here = lax.dynamic_index_in_dim(left_root, slot_id, 0, keepdims=False)
        right_here = lax.dynamic_index_in_dim(right_root, slot_id, 0, keepdims=False)
        left_term = jnp.dot(gradient, gradient.T, preferred_element_type=jnp.float32) * inverse
        right_term = jnp.dot(gradient.T, gradient, preferred_element_type=jnp.float32) * inverse
        right_image = jnp.dot(gradient, right_here, preferred_element_type=jnp.float32).astype(jnp.bfloat16)
        precond = jnp.dot(left_here, right_image, preferred_element_type=jnp.float32).astype(jnp.bfloat16)
        return left_term, right_term, precond

    left_terms, right_terms, precond = lax.map(one_block, (blocks, assignment))
    left_stat = jnp.zeros((SLOT_ALL, BLOCK, BLOCK), jnp.float32).at[assignment].set(left_terms)
    right_stat = jnp.zeros((SLOT_ALL, BLOCK, BLOCK), jnp.float32).at[assignment].set(right_terms)
    whole = precond.reshape(row_slabs, col_blocks, BLOCK, BLOCK).transpose(0, 2, 1, 3).reshape(ROWS, COLS)
    return left_stat, right_stat, whole
```

```python
import jax
import jax.numpy as jnp
from jax import lax
from jax.sharding import Mesh, PartitionSpec as P

Z = ("slab", "half")
F = ("slab", "half", "core")
K = ("half", "core")
T = "plane"


def exchange(array, axes):
    return lax.all_to_all(array, axes, split_axis=0, concat_axis=0, tiled=True)


def dot(a, b, contract):
    return lax.dot_general(a, b, (contract, ((), ())), preferred_element_type=jnp.float32)


def per_device(grads, assignment, left_root, right_root):
    row_dev, col_dev = grads.shape
    slots, stripe, block = right_root.shape
    planes = lax.axis_size(T)
    rings = lax.axis_size(Z)
    owners = 2 * rings
    slabs = rings // 2
    cols = 2 * planes
    tiles = block // row_dev
    rows = row_dev // planes
    slot_all = owners * slots
    here = lax.axis_index(T)
    core = lax.axis_index("core")
    fourth = lax.axis_index(K)
    slab = lax.axis_index("slab")

    grad_all = lax.all_gather(grads, K, axis=0, tiled=True)

    left_rows = lax.dynamic_slice_in_dim(left_root, here * stripe, stripe, 1)
    row_ids = here * stripe + lax.broadcasted_iota(jnp.int32, (stripe, block), 0)
    col_ids = lax.broadcasted_iota(jnp.int32, (stripe, block), 1)
    mixed = jnp.where((col_ids >= row_ids)[None], left_rows, right_root)
    diag = jnp.sum(jnp.where((col_ids == row_ids)[None], right_root, 0), axis=2)
    diag_all = lax.all_gather(diag, F, axis=0, tiled=True)
    halves = mixed.reshape(slots, stripe, 2, block // 2)
    keep = lax.dynamic_index_in_dim(halves, core, 2, keepdims=False)
    send = lax.dynamic_index_in_dim(halves, 1 - core, 2, keepdims=False)
    got = lax.ppermute(send, "core", [(0, 1), (1, 0)])
    first = jnp.where(core == 0, keep, got)
    second = jnp.where(core == 0, got, keep)
    both = jnp.stack([first, second])
    spread_root = (
        both.reshape(2 * slots, stripe, 2, row_dev)
        .transpose(1, 2, 0, 3)
        .reshape(rings, 4 * slots, row_dev)
    )

    mine = exchange(grads.reshape(planes, rows, col_dev), T)
    spread_grad = (
        mine.reshape(planes, rows, 2, tiles, row_dev)
        .transpose(1, 3, 0, 2, 4)
        .reshape(rings, cols, row_dev)
    )
    middle = exchange(jnp.concatenate([spread_root, spread_grad], axis=1), Z)
    middle_root = middle[:, : 4 * slots].reshape(rings, 2, 2 * slots, row_dev)
    middle_grad = middle[:, 4 * slots :].reshape(slabs, 2, cols, row_dev)

    slot_ids = jnp.arange(slot_all, dtype=jnp.int32)
    by_parity = assignment.reshape(slabs, planes, 2).transpose(0, 2, 1).reshape(-1)
    pick_slot = (slot_ids[:, None] == assignment[None, :]).astype(jnp.bfloat16)
    pick_block = (by_parity[:, None] == slot_ids[None, :]).astype(jnp.bfloat16)
    to_slot = [
        dot(pick_slot, middle_grad[:, kk].reshape(slabs * cols, row_dev), ((1,), (0,)))
        .astype(jnp.bfloat16)
        .reshape(owners, slots, row_dev)
        for kk in range(2)
    ]
    to_block = [
        dot(pick_block, middle_root[:, part].reshape(slot_all, row_dev), ((1,), (0,)))
        .astype(jnp.bfloat16)
        .reshape(slabs, 2, 1, planes, row_dev)
        for part in range(2)
    ]
    to_block = jnp.concatenate(to_block, axis=2).reshape(owners, planes, row_dev)
    landed = exchange(jnp.concatenate(to_slot + [to_block], axis=1), F)
    landed_grad = landed[:, : 2 * slots].reshape(rows, tiles, 2, 2, slots, row_dev)
    landed_root = landed[:, 2 * slots :].reshape(rings, 2, planes, row_dev)

    whole_grad = landed_grad.transpose(4, 3, 2, 1, 0, 5).reshape(slots, -1, row_dev)
    whole_grad = jnp.pad(whole_grad, ((0, planes - slots), (0, 0), (0, 0)))
    whole_root = landed_root.transpose(2, 1, 0, 3).reshape(planes, 2 * rings, row_dev)
    grad_rows = whole_grad.shape[1]
    arrived = exchange(jnp.concatenate([whole_grad, whole_root], axis=1), T)
    own = (
        arrived[:, :grad_rows]
        .reshape(planes, 2, 2, tiles, rows, row_dev)
        .transpose(1, 2, 0, 4, 3, 5)
        .reshape(block, block)
    )
    inverse = 1.0 / block
    left_own = (dot(own, own, ((1,), (1,))) * inverse).astype(jnp.bfloat16)
    right_own = (dot(own, own, ((0,), (0,))) * inverse).astype(jnp.bfloat16)
    stats = jnp.stack(
        [left_own.reshape(planes, stripe, block), right_own.reshape(planes, stripe, block)], axis=1
    )
    stats = exchange(stats, T)[:slots].astype(jnp.float32)

    root_all = lax.all_gather(arrived[:, grad_rows:], K, axis=0, tiled=False)
    packed = (
        root_all.reshape(2, 2, planes, 2, stripe, row_dev)
        .transpose(0, 2, 4, 3, 1, 5)
        .reshape(2, block, block)
    )
    slab_assign = lax.dynamic_slice_in_dim(assignment, slab * cols, cols, 0)
    pick_diag = (slab_assign[:, None] == slot_ids[None, :]).astype(jnp.bfloat16)
    diag_slab = dot(pick_diag, diag_all, ((1,), (0,))).astype(jnp.bfloat16)
    diag_planes = lax.all_gather(diag_slab, T, axis=1, tiled=True)
    diag_own = lax.dynamic_slice_in_dim(diag_planes, 2 * here, 2, 0)
    flipped = jnp.swapaxes(packed, 1, 2)
    row_of = lax.broadcasted_iota(jnp.int32, (block, block), 0)
    col_of = lax.broadcasted_iota(jnp.int32, (block, block), 1)
    right_whole = jnp.where((col_of < row_of)[None], packed, flipped)
    right_whole = jnp.where((col_of == row_of)[None], diag_own[:, None, :], right_whole)
    left_whole = jnp.where((col_of >= row_of)[None], packed, flipped)
    left_part = lax.dynamic_slice_in_dim(left_whole, fourth * row_dev, row_dev, 1)
    outs = []
    for part in range(2):
        grad_block = grad_all[:, part * block : (part + 1) * block]
        image = dot(grad_block, right_whole[part], ((1,), (0,))).astype(jnp.bfloat16)
        outs.append(dot(left_part[part], image, ((1,), (0,))).astype(jnp.bfloat16))
    return stats[:, 0], stats[:, 1], jnp.concatenate(outs, axis=1)


def solution(mesh):
    owners, planes = mesh.devices.shape
    fine = Mesh(mesh.devices.reshape(owners // 4, 2, 2, planes), F + (T,))
    in_specs = (P(F, T), P(), P(F, None, None), P(F, T, None))
    out_specs = (P(F, T, None), P(F, T, None), P(F, T))
    return jax.shard_map(
        per_device, mesh=fine, in_specs=in_specs, out_specs=out_specs, check_vma=False
    )
```

```python
import jax
import jax.numpy as jnp
from jax import lax
from jax.experimental import pallas as pl
from jax.experimental.pallas import tpu as pltpu
from jax.sharding import Mesh, PartitionSpec as P

Z = ("slab", "half")
F = ("slab", "half", "core")
K = ("half", "core")
T = "plane"


def exchange(array, axes):
    return lax.all_to_all(array, axes, split_axis=0, concat_axis=0, tiled=True)


def dot(a, b, contract):
    return lax.dot_general(a, b, (contract, ((), ())), preferred_element_type=jnp.float32)


def precondition_kernel(core_ref, own_ref, their_ref, grad_ref, out_ref, packed):
    planes, _, row_dev = own_ref.shape
    block = grad_ref.shape[3]
    stripe = block // planes
    per_tile = row_dev // stripe
    core = core_ref[0]
    for part in range(2):
        own_at = pl.ds(pl.multiple_of((2 * part + core) * row_dev, row_dev), row_dev)
        their_at = pl.ds(pl.multiple_of((2 * part + 1 - core) * row_dev, row_dev), row_dev)
        rows = slice(part * stripe, (part + 1) * stripe)
        for plane in range(planes):
            to = slice(plane * stripe, (plane + 1) * stripe)
            packed[to, own_at] = own_ref[plane, rows, :].astype(jnp.float32)
            packed[to, their_at] = their_ref[plane, rows, :].astype(jnp.float32)
    lane = lax.broadcasted_iota(jnp.int32, (1, row_dev), 1) // stripe
    diag = []
    for tile in range(block // row_dev):
        row = jnp.zeros((1, row_dev), jnp.float32)
        for at in range(per_tile):
            value = own_ref[tile * per_tile + at, 2 * stripe : 2 * stripe + 1, :]
            row = jnp.where(lane == at, value.astype(jnp.float32), row)
        diag.append(row)
    diag = jnp.concatenate(diag, axis=1)
    whole = packed[...]
    flipped = whole.T
    row_of = lax.broadcasted_iota(jnp.int32, (block, block), 0)
    col_of = lax.broadcasted_iota(jnp.int32, (block, block), 1)
    right = jnp.where(col_of < row_of, whole, jnp.where(col_of == row_of, diag, flipped))
    packed[...] = jnp.where(col_of >= row_of, whole, flipped)
    right = right.astype(jnp.bfloat16)
    image = jnp.concatenate(
        [
            jnp.dot(grad_ref[at, part], right, preferred_element_type=jnp.float32).astype(
                jnp.bfloat16
            )
            for part in range(2)
            for at in range(2)
        ]
    )
    for part in range(2):
        at = pl.ds(pl.multiple_of((2 * part + core) * row_dev, row_dev), row_dev)
        left = packed[at, :].astype(jnp.bfloat16)
        out_ref[part] = jnp.dot(left, image, preferred_element_type=jnp.float32).astype(
            jnp.bfloat16
        )


def precondition(core, own, theirs, grad):
    row_dev, block = own.shape[2], grad.shape[3]
    vmem = pl.BlockSpec(memory_space=pltpu.VMEM)
    return pl.pallas_call(
        precondition_kernel,
        out_shape=jax.ShapeDtypeStruct((2, row_dev, block), jnp.bfloat16),
        in_specs=[pl.BlockSpec(memory_space=pltpu.SMEM), vmem, vmem, vmem],
        out_specs=vmem,
        scratch_shapes=[pltpu.VMEM((block, block), jnp.float32)],
        compiler_params=pltpu.CompilerParams(vmem_limit_bytes=32 * 1024 * 1024),
        cost_estimate=pl.CostEstimate(
            flops=3 * block**3, bytes_accessed=4 * block * block, transcendentals=0
        ),
    )(core.reshape(1).astype(jnp.int32), own, theirs, grad)


def per_device(grads, assignment, left_root, right_root):
    row_dev, col_dev = grads.shape
    slots, stripe, block = right_root.shape
    planes = lax.axis_size(T)
    rings = lax.axis_size(Z)
    owners = 2 * rings
    slabs = rings // 2
    cols = 2 * planes
    tiles = block // row_dev
    rows = row_dev // planes
    slot_all = owners * slots
    here = lax.axis_index(T)
    core = lax.axis_index("core")
    half = lax.axis_index("half")

    grad_keep = lax.dynamic_slice_in_dim(grads, half * block, block, 1)
    grad_send = lax.dynamic_slice_in_dim(grads, (1 - half) * block, block, 1)
    grad_got = lax.ppermute(grad_send, "half", [(0, 1), (1, 0)])
    grad_pair = jnp.stack(
        [jnp.where(half == 0, grad_keep, grad_got), jnp.where(half == 0, grad_got, grad_keep)]
    )
    grad_block = lax.all_gather(grad_pair, "core", axis=0, tiled=False)

    def mix(part):
        width = block // 2
        left_rows = lax.dynamic_slice(
            left_root, (0, here * stripe, part * width), (slots, stripe, width)
        )
        right_rows = lax.dynamic_slice_in_dim(right_root, part * width, width, 2)
        row_ids = here * stripe + lax.broadcasted_iota(jnp.int32, (stripe, width), 0)
        col_ids = part * width + lax.broadcasted_iota(jnp.int32, (stripe, width), 1)
        return jnp.where((col_ids >= row_ids)[None], left_rows, right_rows)

    row_ids = here * stripe + lax.broadcasted_iota(jnp.int32, (stripe, block), 0)
    col_ids = lax.broadcasted_iota(jnp.int32, (stripe, block), 1)
    diag = jnp.sum(jnp.where((col_ids == row_ids)[None], right_root, 0), axis=2)
    spread_diag = jnp.pad(diag.T[:, None, :], ((0, 0), (0, 0), (0, row_dev - slots)))
    keep, send = mix(core), mix(1 - core)
    got = lax.ppermute(send, "core", [(0, 1), (1, 0)])
    first = jnp.where(core == 0, keep, got)
    second = jnp.where(core == 0, got, keep)
    both = jnp.stack([first, second])
    spread_root = (
        both.reshape(2 * slots, stripe, 2, row_dev)
        .transpose(1, 2, 0, 3)
        .reshape(rings, 4 * slots, row_dev)
    )

    mine = exchange(grads.reshape(planes, rows, col_dev), T)
    spread_grad = (
        mine.reshape(planes, rows, 2, tiles, row_dev)
        .transpose(1, 3, 0, 2, 4)
        .reshape(rings, cols, row_dev)
    )
    middle = exchange(jnp.concatenate([spread_root, spread_grad, spread_diag], axis=1), Z)
    middle, grad_block = lax.optimization_barrier((middle, grad_block))
    middle_root = middle[:, : 4 * slots].reshape(rings, 2, 2 * slots, row_dev)
    middle_grad = middle[:, 4 * slots : 4 * slots + cols].reshape(slabs, 2, cols, row_dev)

    slot_ids = jnp.arange(slot_all, dtype=jnp.int32)
    by_parity = assignment.reshape(slabs, planes, 2).transpose(0, 2, 1).reshape(-1)
    pick_slot = (slot_ids[:, None] == assignment[None, :]).astype(jnp.bfloat16)
    pick_block = (by_parity[:, None] == slot_ids[None, :]).astype(jnp.bfloat16)
    to_slot = [
        dot(pick_slot, middle_grad[:, kk].reshape(slabs * cols, row_dev), ((1,), (0,)))
        .astype(jnp.bfloat16)
        .reshape(owners, slots, row_dev)
        for kk in range(2)
    ]
    to_block = [
        dot(pick_block, middle_root[:, part].reshape(slot_all, row_dev), ((1,), (0,)))
        .astype(jnp.bfloat16)
        .reshape(slabs, 2, 1, planes, row_dev)
        for part in range(2)
    ]
    to_block = jnp.concatenate(to_block, axis=2).reshape(owners, planes, row_dev)
    block_ring = by_parity // (2 * slots)
    block_slot = jnp.where(by_parity // slots % 2 == core, by_parity % slots, -1)
    pick_ring = (block_ring[:, None] == jnp.arange(rings)[None, :]).astype(jnp.bfloat16)
    ring_diag = dot(pick_ring, middle[:, 4 * slots + cols], ((1,), (0,)))
    lanes = jnp.arange(row_dev, dtype=jnp.int32)
    to_diag = jnp.sum(jnp.where(block_slot[:, None] == lanes[None, :], ring_diag, 0), axis=1)
    to_diag = to_diag.astype(jnp.bfloat16).reshape(slabs * 2, 1, 1, planes)
    to_diag = jnp.pad(to_diag, ((0, 0), (0, 0), (0, 0), (0, row_dev - planes)))
    to_diag = jnp.broadcast_to(to_diag, (slabs * 2, 2, 1, row_dev)).reshape(owners, 1, row_dev)
    landed = exchange(jnp.concatenate(to_slot + [to_block, to_diag], axis=1), F)
    landed_grad = landed[:, : 2 * slots].reshape(rows, tiles, 2, 2, slots, row_dev)
    landed_root = landed[:, 2 * slots : 2 * slots + planes].reshape(rings, 2, planes, row_dev)

    whole_grad = landed_grad.transpose(4, 3, 2, 1, 0, 5).reshape(slots, -1, row_dev)
    whole_grad = jnp.pad(whole_grad, ((0, planes - slots), (0, 0), (0, 0)))
    whole_root = landed_root.transpose(2, 1, 0, 3).reshape(planes, 2 * rings, row_dev)
    landed_diag = landed[:, 2 * slots + planes, :planes].reshape(rings, 2, planes)
    whole_diag = jnp.tile((landed_diag[:, 0] + landed_diag[:, 1]).T, (1, row_dev // stripe))
    whole_diag = jnp.pad(whole_diag[:, None, :], ((0, 0), (0, 7), (0, 0)))
    grad_rows = whole_grad.shape[1]
    arrived = exchange(jnp.concatenate([whole_grad, whole_root, whole_diag], axis=1), T)
    own = (
        arrived[:, :grad_rows]
        .reshape(planes, 2, 2, tiles, rows, row_dev)
        .transpose(1, 2, 0, 4, 3, 5)
        .reshape(block, block)
    )
    inverse = 1.0 / block
    left_own = (dot(own, own, ((1,), (1,))) * inverse).astype(jnp.bfloat16)
    right_own = (dot(own, own, ((0,), (0,))) * inverse).astype(jnp.bfloat16)
    stats = jnp.stack(
        [left_own.reshape(planes, stripe, block), right_own.reshape(planes, stripe, block)], axis=1
    )
    stats = exchange(stats, T)[:slots].astype(jnp.float32)

    own_root = arrived[:, grad_rows:]
    their_root = lax.ppermute(own_root, "core", [(0, 1), (1, 0)])
    ready = precondition(core, own_root, their_root, grad_block)
    keep = lax.dynamic_index_in_dim(ready, half, 0, keepdims=False)
    send = lax.dynamic_index_in_dim(ready, 1 - half, 0, keepdims=False)
    got = lax.ppermute(send, "half", [(0, 1), (1, 0)])
    first = jnp.where(half == 0, keep, got)
    second = jnp.where(half == 0, got, keep)
    return stats[:, 0], stats[:, 1], jnp.concatenate([first, second], axis=1)


def solution(mesh):
    owners, planes = mesh.devices.shape
    fine = Mesh(mesh.devices.reshape(owners // 4, 2, 2, planes), F + (T,))
    in_specs = (P(F, T), P(), P(F, None, None), P(F, T, None))
    out_specs = (P(F, T, None), P(F, T, None), P(F, T))
    return jax.shard_map(
        per_device, mesh=fine, in_specs=in_specs, out_specs=out_specs, check_vma=False
    )
```

```python
import jax
import jax.numpy as jnp
from jax import lax
from jax.experimental import pallas as pl
from jax.experimental.pallas import tpu as pltpu
from jax.sharding import Mesh, PartitionSpec as P

Z = ("slab", "half")
F = ("slab", "half", "core")
K = ("half", "core")
T = "plane"


def exchange(array, axes):
    return lax.all_to_all(array, axes, split_axis=0, concat_axis=0, tiled=True)


def dot(a, b, contract):
    return lax.dot_general(a, b, (contract, ((), ())), preferred_element_type=jnp.float32)


def precondition_kernel(core_ref, own_ref, their_ref, grad_ref, out_ref, packed):
    planes, _, row_dev = own_ref.shape
    block = grad_ref.shape[3]
    stripe = block // planes
    per_tile = row_dev // stripe
    core = core_ref[0]
    for part in range(2):
        own_at = pl.ds(pl.multiple_of((2 * part + core) * row_dev, row_dev), row_dev)
        their_at = pl.ds(pl.multiple_of((2 * part + 1 - core) * row_dev, row_dev), row_dev)
        rows = slice(part * stripe, (part + 1) * stripe)
        for plane in range(planes):
            to = slice(plane * stripe, (plane + 1) * stripe)
            packed[to, own_at] = own_ref[plane, rows, :].astype(jnp.float32)
            packed[to, their_at] = their_ref[plane, rows, :].astype(jnp.float32)
    lane = lax.broadcasted_iota(jnp.int32, (1, row_dev), 1) // stripe
    diag = []
    for tile in range(block // row_dev):
        row = jnp.zeros((1, row_dev), jnp.float32)
        for at in range(per_tile):
            value = own_ref[tile * per_tile + at, 2 * stripe : 2 * stripe + 1, :]
            row = jnp.where(lane == at, value.astype(jnp.float32), row)
        diag.append(row)
    diag = jnp.concatenate(diag, axis=1)
    whole = packed[...]
    flipped = whole.T
    row_of = lax.broadcasted_iota(jnp.int32, (block, block), 0)
    col_of = lax.broadcasted_iota(jnp.int32, (block, block), 1)
    right = jnp.where(col_of < row_of, whole, jnp.where(col_of == row_of, diag, flipped))
    packed[...] = jnp.where(col_of >= row_of, whole, flipped)
    right = right.astype(jnp.bfloat16)
    image = jnp.concatenate(
        [
            jnp.dot(grad_ref[at, part], right, preferred_element_type=jnp.float32).astype(
                jnp.bfloat16
            )
            for part in range(2)
            for at in range(2)
        ]
    )
    for part in range(2):
        at = pl.ds(pl.multiple_of((2 * part + core) * row_dev, row_dev), row_dev)
        left = packed[at, :].astype(jnp.bfloat16)
        out_ref[part] = jnp.dot(left, image, preferred_element_type=jnp.float32).astype(
            jnp.bfloat16
        )


def precondition(core, own, theirs, grad):
    row_dev, block = own.shape[2], grad.shape[3]
    vmem = pl.BlockSpec(memory_space=pltpu.VMEM)
    return pl.pallas_call(
        precondition_kernel,
        out_shape=jax.ShapeDtypeStruct((2, row_dev, block), jnp.bfloat16),
        in_specs=[pl.BlockSpec(memory_space=pltpu.SMEM), vmem, vmem, vmem],
        out_specs=vmem,
        scratch_shapes=[pltpu.VMEM((block, block), jnp.float32)],
        compiler_params=pltpu.CompilerParams(vmem_limit_bytes=32 * 1024 * 1024),
        cost_estimate=pl.CostEstimate(
            flops=3 * block**3, bytes_accessed=4 * block * block, transcendentals=0
        ),
    )(core.reshape(1).astype(jnp.int32), own, theirs, grad)


def per_device(grads, assignment, left_root, right_root):
    row_dev, col_dev = grads.shape
    slots, stripe, block = right_root.shape
    planes = lax.axis_size(T)
    rings = lax.axis_size(Z)
    owners = 2 * rings
    slabs = rings // 2
    cols = 2 * planes
    tiles = block // row_dev
    rows = row_dev // planes
    slot_all = owners * slots
    here = lax.axis_index(T)
    core = lax.axis_index("core")
    half = lax.axis_index("half")

    row_ids = here * stripe + lax.broadcasted_iota(jnp.int32, (stripe, block), 0)
    col_ids = lax.broadcasted_iota(jnp.int32, (stripe, block), 1)
    left_rows = lax.dynamic_slice_in_dim(left_root, here * stripe, stripe, 1)
    mixed = jnp.where((col_ids >= row_ids)[None], left_rows, right_root)
    diag = jnp.sum(jnp.where((col_ids == row_ids)[None], right_root, 0), axis=2)
    by_slab = assignment.reshape(slabs, cols)
    owner_of = by_slab // slots
    same = owner_of[:, :, None] == owner_of[:, None, :]
    before = jnp.arange(cols)[None, :] < jnp.arange(cols)[:, None]
    rank = jnp.sum((same & before[None]).astype(jnp.int32), axis=2)
    mine_at = owner_of == lax.axis_index(F)
    place = jnp.arange(2, dtype=jnp.int32)
    at_place = mine_at[:, None, :] & (rank[:, None, :] == place[None, :, None])
    slot_at = jnp.sum(jnp.where(at_place, by_slab[:, None, :] % slots + 1, 0), axis=2) - 1
    pick_diag = (slot_at.reshape(-1, 1) == jnp.arange(slots)[None, :]).astype(jnp.bfloat16)
    to_diag = dot(pick_diag, diag, ((1,), (0,))).astype(jnp.bfloat16).reshape(slabs, 2 * stripe)
    to_diag = jnp.pad(to_diag, ((0, 0), (0, row_dev - 2 * stripe)))
    to_diag = jnp.broadcast_to(to_diag[:, None, None, :], (slabs, 4, 1, row_dev))
    to_diag = to_diag.reshape(owners, 1, row_dev)
    both = lax.all_gather(mixed, "core", axis=0, tiled=False)
    both = lax.dynamic_slice_in_dim(both, core * (block // 2), block // 2, 3)
    spread_root = (
        both.reshape(2, slots, stripe, 2, row_dev)
        .transpose(2, 1, 0, 3, 4)
        .reshape(rings, slots, 4, row_dev)
    )

    mine = exchange(grads.reshape(planes, rows, col_dev), T)
    spread_grad = (
        mine.reshape(planes, rows, 2, tiles, row_dev)
        .transpose(1, 3, 0, 2, 4)
        .reshape(rings, cols // 4, 4, row_dev)
    )
    middle = exchange(jnp.concatenate([spread_root, spread_grad], axis=1), Z)
    middle_root = middle[:, :slots].reshape(4 * slots * rings, row_dev)
    middle_grad = middle[:, slots:].reshape(cols * rings, row_dev)

    ids = jnp.arange(slot_all, dtype=jnp.int32).reshape(rings, 2, slots)
    pair = jnp.arange(2, dtype=jnp.int32)
    table = assignment.reshape(slabs, planes, 2)
    root_have = ids.transpose(0, 2, 1)[..., None] * 2 + pair
    root_want = table.transpose(0, 2, 1)[:, :, None, :] * 2 + pair[None, None, :, None]
    grad_have = table.reshape(slabs, 1, cols) * 2 + pair[None, :, None]
    grad_want = ids.reshape(owners, 1, slots) * 2 + pair[None, :, None]

    def pick(want, have, values):
        chosen = (want.reshape(-1, 1) == have.reshape(1, -1)).astype(jnp.bfloat16)
        return dot(chosen, values, ((1,), (0,))).astype(jnp.bfloat16)

    to_slot = pick(grad_want, grad_have, middle_grad).reshape(owners, 2 * slots, row_dev)
    to_block = pick(root_want, root_have, middle_root).reshape(owners, planes, row_dev)
    landed = exchange(jnp.concatenate([to_slot, to_block, to_diag], axis=1), F)
    landed, late = lax.optimization_barrier((landed, grads))

    grad_keep = lax.dynamic_slice_in_dim(late, half * block, block, 1)
    grad_send = lax.dynamic_slice_in_dim(late, (1 - half) * block, block, 1)
    grad_got = lax.ppermute(grad_send, "half", [(0, 1), (1, 0)])
    grad_pair = jnp.stack(
        [jnp.where(half == 0, grad_keep, grad_got), jnp.where(half == 0, grad_got, grad_keep)]
    )
    grad_block = lax.all_gather(grad_pair, "core", axis=0, tiled=False)

    landed_grad = landed[:, : 2 * slots].reshape(rows, tiles, 2, 2, slots, row_dev)
    landed_root = landed[:, 2 * slots : 2 * slots + planes].reshape(rings, 2, planes, row_dev)

    whole_grad = landed_grad.transpose(4, 3, 2, 1, 0, 5).reshape(slots, -1, row_dev)
    whole_grad = jnp.pad(whole_grad, ((0, planes - slots), (0, 0), (0, 0)))
    whole_root = landed_root.transpose(2, 1, 0, 3).reshape(planes, 2 * rings, row_dev)
    slab = lax.axis_index("slab")
    own_cols = lax.dynamic_index_in_dim(owner_of.reshape(slabs, planes, 2), slab, 0, False)
    own_cols = lax.dynamic_index_in_dim(own_cols, half, 1, False)
    own_rank = lax.dynamic_index_in_dim(rank.reshape(slabs, planes, 2), slab, 0, False)
    own_rank = lax.dynamic_index_in_dim(own_rank, half, 1, False)
    landed_diag = landed[:, 2 * slots + planes]
    from_owner = own_cols[:, None] == jnp.arange(owners)[None, :]
    whole_diag = sum(
        dot(
            (from_owner & (own_rank == at)[:, None]).astype(jnp.bfloat16),
            landed_diag[:, at * stripe : (at + 1) * stripe],
            ((1,), (0,)),
        )
        for at in range(2)
    )
    whole_diag = jnp.tile(whole_diag.astype(jnp.bfloat16), (1, row_dev // stripe))
    whole_diag = jnp.pad(whole_diag[:, None, :], ((0, 0), (0, 7), (0, 0)))
    grad_rows = whole_grad.shape[1]
    arrived = exchange(jnp.concatenate([whole_grad, whole_root, whole_diag], axis=1), T)
    own = (
        arrived[:, :grad_rows]
        .reshape(planes, 2, 2, tiles, rows, row_dev)
        .transpose(1, 2, 0, 4, 3, 5)
        .reshape(block, block)
    )
    inverse = 1.0 / block
    left_own = (dot(own, own, ((1,), (1,))) * inverse).astype(jnp.bfloat16)
    right_own = (dot(own, own, ((0,), (0,))) * inverse).astype(jnp.bfloat16)
    stats = jnp.stack(
        [left_own.reshape(planes, stripe, block), right_own.reshape(planes, stripe, block)], axis=1
    )
    own_root = arrived[:, grad_rows:]
    own_root, stats = lax.optimization_barrier((own_root, stats))
    stats = exchange(stats, T)[:slots].astype(jnp.float32)

    their_root = lax.ppermute(own_root, "core", [(0, 1), (1, 0)])
    ready = precondition(core, own_root, their_root, grad_block)
    keep = lax.dynamic_index_in_dim(ready, half, 0, keepdims=False)
    send = lax.dynamic_index_in_dim(ready, 1 - half, 0, keepdims=False)
    got = lax.ppermute(send, "half", [(0, 1), (1, 0)])
    first = jnp.where(half == 0, keep, got)
    second = jnp.where(half == 0, got, keep)
    return stats[:, 0], stats[:, 1], jnp.concatenate([first, second], axis=1)


def solution(mesh):
    owners, planes = mesh.devices.shape
    fine = Mesh(mesh.devices.reshape(owners // 4, 2, 2, planes), F + (T,))
    in_specs = (P(F, T), P(), P(F, None, None), P(F, T, None))
    out_specs = (P(F, T, None), P(F, T, None), P(F, T))
    return jax.shard_map(
        per_device, mesh=fine, in_specs=in_specs, out_specs=out_specs, check_vma=False
    )
```

```python
import jax
import jax.numpy as jnp
from jax import lax
from jax.experimental import pallas as pl
from jax.experimental.pallas import tpu as pltpu
from jax.sharding import Mesh, PartitionSpec as P

Z = ("slab", "half")
F = ("slab", "half", "core")
K = ("half", "core")
T = "plane"


def exchange(array, axes):
    return lax.all_to_all(array, axes, split_axis=0, concat_axis=0, tiled=True)


def ring_exchange(array, axes):
    count = array.shape[0]
    order = [(at + count // 2) % count for at in range(count)]
    return lax.all_to_all(
        array, axes, split_axis=0, concat_axis=0, tiled=True, axis_index_groups=[order]
    )


def half_turn(array):
    return jnp.roll(array, array.shape[0] // 2, axis=0)


def dot(a, b, contract):
    return lax.dot_general(a, b, (contract, ((), ())), preferred_element_type=jnp.float32)


def precondition_kernel(core_ref, own_ref, their_ref, grad_ref, out_ref, packed):
    planes, _, row_dev = own_ref.shape
    block = grad_ref.shape[3]
    stripe = block // planes
    per_tile = row_dev // stripe
    core = core_ref[0]
    for part in range(2):
        own_at = pl.ds(pl.multiple_of((2 * part + core) * row_dev, row_dev), row_dev)
        their_at = pl.ds(pl.multiple_of((2 * part + 1 - core) * row_dev, row_dev), row_dev)
        rows = slice(part * stripe, (part + 1) * stripe)
        for plane in range(planes):
            to = slice(plane * stripe, (plane + 1) * stripe)
            packed[to, own_at] = own_ref[plane, rows, :].astype(jnp.float32)
            packed[to, their_at] = their_ref[plane, rows, :].astype(jnp.float32)
    lane = lax.broadcasted_iota(jnp.int32, (1, row_dev), 1) // stripe
    diag = []
    for tile in range(block // row_dev):
        row = jnp.zeros((1, row_dev), jnp.float32)
        for at in range(per_tile):
            value = own_ref[tile * per_tile + at, 2 * stripe : 2 * stripe + 1, :]
            row = jnp.where(lane == at, value.astype(jnp.float32), row)
        diag.append(row)
    diag = jnp.concatenate(diag, axis=1)
    whole = packed[...]
    flipped = whole.T
    row_of = lax.broadcasted_iota(jnp.int32, (block, block), 0)
    col_of = lax.broadcasted_iota(jnp.int32, (block, block), 1)
    right = jnp.where(col_of < row_of, whole, jnp.where(col_of == row_of, diag, flipped))
    packed[...] = jnp.where(col_of >= row_of, whole, flipped)
    right = right.astype(jnp.bfloat16)
    image = jnp.concatenate(
        [
            jnp.dot(grad_ref[at, part], right, preferred_element_type=jnp.float32).astype(
                jnp.bfloat16
            )
            for part in range(2)
            for at in range(2)
        ]
    )
    for part in range(2):
        at = pl.ds(pl.multiple_of((2 * part + core) * row_dev, row_dev), row_dev)
        left = packed[at, :].astype(jnp.bfloat16)
        out_ref[part] = jnp.dot(left, image, preferred_element_type=jnp.float32).astype(
            jnp.bfloat16
        )


def precondition(core, own, theirs, grad):
    row_dev, block = own.shape[2], grad.shape[3]
    vmem = pl.BlockSpec(memory_space=pltpu.VMEM)
    return pl.pallas_call(
        precondition_kernel,
        out_shape=jax.ShapeDtypeStruct((2, row_dev, block), jnp.bfloat16),
        in_specs=[pl.BlockSpec(memory_space=pltpu.SMEM), vmem, vmem, vmem],
        out_specs=vmem,
        scratch_shapes=[pltpu.VMEM((block, block), jnp.float32)],
        compiler_params=pltpu.CompilerParams(vmem_limit_bytes=32 * 1024 * 1024),
        cost_estimate=pl.CostEstimate(
            flops=3 * block**3, bytes_accessed=4 * block * block, transcendentals=0
        ),
    )(core.reshape(1).astype(jnp.int32), own, theirs, grad)


def per_device(grads, assignment, left_root, right_root):
    row_dev, col_dev = grads.shape
    slots, stripe, block = right_root.shape
    planes = lax.axis_size(T)
    rings = lax.axis_size(Z)
    owners = 2 * rings
    slabs = rings // 2
    cols = 2 * planes
    tiles = block // row_dev
    rows = row_dev // planes
    slot_all = owners * slots
    here = lax.axis_index(T)
    core = lax.axis_index("core")
    half = lax.axis_index("half")

    row_ids = here * stripe + lax.broadcasted_iota(jnp.int32, (stripe, block), 0)
    col_ids = lax.broadcasted_iota(jnp.int32, (stripe, block), 1)
    left_rows = lax.dynamic_slice_in_dim(left_root, here * stripe, stripe, 1)
    mixed = jnp.where((col_ids >= row_ids)[None], left_rows, right_root)
    diag = jnp.sum(jnp.where((col_ids == row_ids)[None], right_root, 0), axis=2)
    by_slab = assignment.reshape(slabs, cols)
    owner_of = by_slab // slots
    same = owner_of[:, :, None] == owner_of[:, None, :]
    before = jnp.arange(cols)[None, :] < jnp.arange(cols)[:, None]
    rank = jnp.sum((same & before[None]).astype(jnp.int32), axis=2)
    mine_at = owner_of == lax.axis_index(F)
    place = jnp.arange(2, dtype=jnp.int32)
    at_place = mine_at[:, None, :] & (rank[:, None, :] == place[None, :, None])
    slot_at = jnp.sum(jnp.where(at_place, by_slab[:, None, :] % slots + 1, 0), axis=2) - 1
    pick_diag = (half_turn(slot_at).reshape(-1, 1) == jnp.arange(slots)[None, :]).astype(jnp.bfloat16)
    to_diag = dot(pick_diag, diag, ((1,), (0,))).astype(jnp.bfloat16).reshape(slabs, 2 * stripe)
    to_diag = jnp.pad(to_diag, ((0, 0), (0, row_dev - 2 * stripe)))
    to_diag = jnp.broadcast_to(to_diag[:, None, None, :], (slabs, 4, 1, row_dev))
    to_diag = to_diag.reshape(owners, 1, row_dev)
    both = lax.all_gather(mixed, "core", axis=0, tiled=False)
    both = lax.dynamic_slice_in_dim(both, core * (block // 2), block // 2, 3)
    spread_root = (
        both.reshape(2, slots, stripe, 2, row_dev)
        .transpose(2, 1, 0, 3, 4)
        .reshape(rings, slots, 4, row_dev)
    )

    mine = exchange(grads.reshape(planes, rows, col_dev), T)
    spread_grad = (
        mine.reshape(planes, rows, 2, tiles, row_dev)
        .transpose(1, 3, 0, 2, 4)
        .reshape(rings, cols // 4, 4, row_dev)
    )
    middle = ring_exchange(jnp.concatenate([spread_root, spread_grad], axis=1), Z)
    middle_root = middle[:, :slots].reshape(4 * slots * rings, row_dev)
    middle_grad = middle[:, slots:].reshape(cols * rings, row_dev)

    ids = half_turn(jnp.arange(slot_all, dtype=jnp.int32).reshape(rings, 2, slots))
    pair = jnp.arange(2, dtype=jnp.int32)
    table = half_turn(assignment.reshape(slabs, planes, 2))
    root_have = ids.transpose(0, 2, 1)[..., None] * 2 + pair
    root_want = table.transpose(0, 2, 1)[:, :, None, :] * 2 + pair[None, None, :, None]
    grad_have = table.reshape(slabs, 1, cols) * 2 + pair[None, :, None]
    grad_want = ids.reshape(owners, 1, slots) * 2 + pair[None, :, None]

    def pick(want, have, values):
        chosen = (want.reshape(-1, 1) == have.reshape(1, -1)).astype(jnp.bfloat16)
        return dot(chosen, values, ((1,), (0,))).astype(jnp.bfloat16)

    to_slot = pick(grad_want, grad_have, middle_grad).reshape(owners, 2 * slots, row_dev)
    to_block = pick(root_want, root_have, middle_root).reshape(owners, planes, row_dev)
    landed = ring_exchange(jnp.concatenate([to_slot, to_block, to_diag], axis=1), F)
    landed, late = lax.optimization_barrier((landed, grads))

    grad_keep = lax.dynamic_slice_in_dim(late, half * block, block, 1)
    grad_send = lax.dynamic_slice_in_dim(late, (1 - half) * block, block, 1)
    grad_got = lax.ppermute(grad_send, "half", [(0, 1), (1, 0)])
    grad_pair = jnp.stack(
        [jnp.where(half == 0, grad_keep, grad_got), jnp.where(half == 0, grad_got, grad_keep)]
    )
    grad_block = lax.all_gather(grad_pair, "core", axis=0, tiled=False)

    landed_grad = landed[:, : 2 * slots].reshape(rows, tiles, 2, 2, slots, row_dev)
    landed_root = landed[:, 2 * slots : 2 * slots + planes].reshape(rings, 2, planes, row_dev)

    whole_grad = landed_grad.transpose(4, 3, 2, 1, 0, 5).reshape(slots, -1, row_dev)
    whole_grad = jnp.pad(whole_grad, ((0, planes - slots), (0, 0), (0, 0)))
    whole_root = landed_root.transpose(2, 1, 0, 3).reshape(planes, 2 * rings, row_dev)
    slab = lax.axis_index("slab")
    own_cols = lax.dynamic_index_in_dim(owner_of.reshape(slabs, planes, 2), slab, 0, False)
    own_cols = lax.dynamic_index_in_dim(own_cols, half, 1, False)
    own_rank = lax.dynamic_index_in_dim(rank.reshape(slabs, planes, 2), slab, 0, False)
    own_rank = lax.dynamic_index_in_dim(own_rank, half, 1, False)
    landed_diag = landed[:, 2 * slots + planes]
    from_owner = own_cols[:, None] == half_turn(jnp.arange(owners))[None, :]
    whole_diag = sum(
        dot(
            (from_owner & (own_rank == at)[:, None]).astype(jnp.bfloat16),
            landed_diag[:, at * stripe : (at + 1) * stripe],
            ((1,), (0,)),
        )
        for at in range(2)
    )
    whole_diag = jnp.tile(whole_diag.astype(jnp.bfloat16), (1, row_dev // stripe))
    whole_diag = jnp.pad(whole_diag[:, None, :], ((0, 0), (0, 7), (0, 0)))
    grad_rows = whole_grad.shape[1]
    arrived = exchange(jnp.concatenate([whole_grad, whole_root, whole_diag], axis=1), T)
    own = (
        arrived[:, :grad_rows]
        .reshape(planes, 2, 2, tiles, rows, row_dev)
        .transpose(1, 2, 0, 4, 3, 5)
        .reshape(block, block)
    )
    inverse = 1.0 / block
    left_own = (dot(own, own, ((1,), (1,))) * inverse).astype(jnp.bfloat16)
    right_own = (dot(own, own, ((0,), (0,))) * inverse).astype(jnp.bfloat16)
    stats = jnp.stack(
        [left_own.reshape(planes, stripe, block), right_own.reshape(planes, stripe, block)], axis=1
    )
    own_root = arrived[:, grad_rows:]
    own_root, stats = lax.optimization_barrier((own_root, stats))
    stats = exchange(stats, T)[:slots].astype(jnp.float32)

    their_root = lax.ppermute(own_root, "core", [(0, 1), (1, 0)])
    ready = precondition(core, own_root, their_root, grad_block)
    keep = lax.dynamic_index_in_dim(ready, half, 0, keepdims=False)
    send = lax.dynamic_index_in_dim(ready, 1 - half, 0, keepdims=False)
    got = lax.ppermute(send, "half", [(0, 1), (1, 0)])
    first = jnp.where(half == 0, keep, got)
    second = jnp.where(half == 0, got, keep)
    return stats[:, 0], stats[:, 1], jnp.concatenate([first, second], axis=1)


def solution(mesh):
    owners, planes = mesh.devices.shape
    fine = Mesh(mesh.devices.reshape(owners // 4, 2, 2, planes), F + (T,))
    in_specs = (P(F, T), P(), P(F, None, None), P(F, T, None))
    out_specs = (P(F, T, None), P(F, T, None), P(F, T))
    return jax.shard_map(
        per_device, mesh=fine, in_specs=in_specs, out_specs=out_specs, check_vma=False
    )
```

```python
import jax
import jax.numpy as jnp
from jax import lax
from jax.experimental import pallas as pl
from jax.experimental.pallas import tpu as pltpu
from jax.sharding import Mesh, PartitionSpec as P

Z = ("slab", "half")
F = ("slab", "half", "core")
K = ("half", "core")
T = "plane"


def exchange(array, axes):
    return lax.all_to_all(array, axes, split_axis=0, concat_axis=0, tiled=True)


def ring_exchange(array, axes):
    count = array.shape[0]
    order = [(at + count // 2) % count for at in range(count)]
    return lax.all_to_all(
        array, axes, split_axis=0, concat_axis=0, tiled=True, axis_index_groups=[order]
    )


def half_turn(array):
    return jnp.roll(array, array.shape[0] // 2, axis=0)


def dot(a, b, contract):
    return lax.dot_general(a, b, (contract, ((), ())), preferred_element_type=jnp.float32)


def precondition_kernel(core_ref, own_ref, their_ref, grad_ref, out_ref, packed):
    planes, _, row_dev = own_ref.shape
    block = grad_ref.shape[3]
    stripe = block // planes
    per_tile = row_dev // stripe
    core = core_ref[0]
    for part in range(2):
        own_at = pl.ds(pl.multiple_of((2 * part + core) * row_dev, row_dev), row_dev)
        their_at = pl.ds(pl.multiple_of((2 * part + 1 - core) * row_dev, row_dev), row_dev)
        rows = slice(part * stripe, (part + 1) * stripe)
        for plane in range(planes):
            to = slice(plane * stripe, (plane + 1) * stripe)
            packed[to, own_at] = own_ref[plane, rows, :].astype(jnp.float32)
            packed[to, their_at] = their_ref[plane, rows, :].astype(jnp.float32)
    lane = lax.broadcasted_iota(jnp.int32, (1, row_dev), 1) // stripe
    diag = []
    for tile in range(block // row_dev):
        row = jnp.zeros((1, row_dev), jnp.float32)
        for at in range(per_tile):
            value = own_ref[tile * per_tile + at, 2 * stripe : 2 * stripe + 1, :]
            row = jnp.where(lane == at, value.astype(jnp.float32), row)
        diag.append(row)
    diag = jnp.concatenate(diag, axis=1)
    whole = packed[...]
    flipped = whole.T
    row_of = lax.broadcasted_iota(jnp.int32, (block, block), 0)
    col_of = lax.broadcasted_iota(jnp.int32, (block, block), 1)
    right = jnp.where(col_of < row_of, whole, jnp.where(col_of == row_of, diag, flipped))
    packed[...] = jnp.where(col_of >= row_of, whole, flipped)
    right = right.astype(jnp.bfloat16)
    image = jnp.concatenate(
        [
            jnp.dot(grad_ref[at, part], right, preferred_element_type=jnp.float32).astype(
                jnp.bfloat16
            )
            for part in range(2)
            for at in range(2)
        ]
    )
    for part in range(2):
        at = pl.ds(pl.multiple_of((2 * part + core) * row_dev, row_dev), row_dev)
        left = packed[at, :].astype(jnp.bfloat16)
        out_ref[part] = jnp.dot(left, image, preferred_element_type=jnp.float32).astype(
            jnp.bfloat16
        )


def precondition(core, own, theirs, grad):
    row_dev, block = own.shape[2], grad.shape[3]
    vmem = pl.BlockSpec(memory_space=pltpu.VMEM)
    return pl.pallas_call(
        precondition_kernel,
        out_shape=jax.ShapeDtypeStruct((2, row_dev, block), jnp.bfloat16),
        in_specs=[pl.BlockSpec(memory_space=pltpu.SMEM), vmem, vmem, vmem],
        out_specs=vmem,
        scratch_shapes=[pltpu.VMEM((block, block), jnp.float32)],
        compiler_params=pltpu.CompilerParams(vmem_limit_bytes=32 * 1024 * 1024),
        cost_estimate=pl.CostEstimate(
            flops=3 * block**3, bytes_accessed=4 * block * block, transcendentals=0
        ),
    )(core.reshape(1).astype(jnp.int32), own, theirs, grad)


def per_device(grads, assignment, left_root, right_root):
    row_dev, col_dev = grads.shape
    slots, stripe, block = right_root.shape
    planes = lax.axis_size(T)
    rings = lax.axis_size(Z)
    owners = 2 * rings
    slabs = rings // 2
    cols = 2 * planes
    tiles = block // row_dev
    rows = row_dev // planes
    slot_all = owners * slots
    here = lax.axis_index(T)
    core = lax.axis_index("core")
    half = lax.axis_index("half")

    row_ids = here * stripe + lax.broadcasted_iota(jnp.int32, (stripe, block), 0)
    col_ids = lax.broadcasted_iota(jnp.int32, (stripe, block), 1)
    left_rows = lax.dynamic_slice_in_dim(left_root, here * stripe, stripe, 1)
    mixed = jnp.where((col_ids >= row_ids)[None], left_rows, right_root)
    diag = jnp.sum(jnp.where((col_ids == row_ids)[None], right_root, 0), axis=2)
    by_slab = assignment.reshape(slabs, cols)
    owner_of = by_slab // slots
    same = owner_of[:, :, None] == owner_of[:, None, :]
    before = jnp.arange(cols)[None, :] < jnp.arange(cols)[:, None]
    rank = jnp.sum((same & before[None]).astype(jnp.int32), axis=2)
    mine_at = owner_of == lax.axis_index(F)
    place = jnp.arange(2, dtype=jnp.int32)
    at_place = mine_at[:, None, :] & (rank[:, None, :] == place[None, :, None])
    slot_at = jnp.sum(jnp.where(at_place, by_slab[:, None, :] % slots + 1, 0), axis=2) - 1
    pick_diag = (half_turn(slot_at).reshape(-1, 1) == jnp.arange(slots)[None, :]).astype(jnp.bfloat16)
    to_diag = dot(pick_diag, diag, ((1,), (0,))).astype(jnp.bfloat16).reshape(slabs, 2 * stripe)
    to_diag = jnp.pad(to_diag, ((0, 0), (0, row_dev - 2 * stripe)))
    to_diag = jnp.broadcast_to(to_diag[:, None, None, :], (slabs, 4, 1, row_dev))
    to_diag = to_diag.reshape(owners, 1, row_dev)
    both = lax.all_gather(mixed, "core", axis=0, tiled=False)
    both = lax.dynamic_slice_in_dim(both, core * (block // 2), block // 2, 3)
    spread_root = (
        both.reshape(2, slots, stripe, 2, row_dev)
        .transpose(2, 1, 0, 3, 4)
        .reshape(rings, slots, 4, row_dev)
    )

    mine = exchange(grads.reshape(planes, rows, col_dev), T)
    spread_grad = (
        mine.reshape(planes, rows, 2, tiles, row_dev)
        .transpose(1, 3, 0, 2, 4)
        .reshape(rings, cols // 4, 4, row_dev)
    )
    middle = ring_exchange(jnp.concatenate([spread_root, spread_grad], axis=1), Z)
    middle_root = middle[:, :slots].reshape(4 * slots * rings, row_dev)
    middle_grad = middle[:, slots:].reshape(slabs, 2, cols, row_dev)

    ids = half_turn(jnp.arange(slot_all, dtype=jnp.int32).reshape(rings, 2, slots))
    pair = jnp.arange(2, dtype=jnp.int32)
    table = half_turn(assignment.reshape(slabs, planes, 2))
    root_have = ids.transpose(0, 2, 1)[..., None] * 2 + pair
    root_want = table.transpose(0, 2, 1)[:, :, None, :] * 2 + pair[None, None, :, None]

    def pick(want, have, values):
        chosen = (want.reshape(-1, 1) == have.reshape(1, -1)).astype(jnp.bfloat16)
        return dot(chosen, values, ((1,), (0,))).astype(jnp.bfloat16)

    to_slot = [
        pick(ids, table, middle_grad[:, kk].reshape(slabs * cols, row_dev)).reshape(
            owners, slots, row_dev
        )
        for kk in range(2)
    ]
    to_block = pick(root_want, root_have, middle_root).reshape(owners, planes, row_dev)
    landed = ring_exchange(jnp.concatenate(to_slot + [to_block, to_diag], axis=1), F)
    landed, late = lax.optimization_barrier((landed, grads))

    grad_keep = lax.dynamic_slice_in_dim(late, half * block, block, 1)
    grad_send = lax.dynamic_slice_in_dim(late, (1 - half) * block, block, 1)
    grad_got = lax.ppermute(grad_send, "half", [(0, 1), (1, 0)])
    grad_pair = jnp.stack(
        [jnp.where(half == 0, grad_keep, grad_got), jnp.where(half == 0, grad_got, grad_keep)]
    )
    grad_block = lax.all_gather(grad_pair, "core", axis=0, tiled=False)

    landed_grad = landed[:, : 2 * slots].reshape(rows, tiles, 2, 2, slots, row_dev)
    landed_root = landed[:, 2 * slots : 2 * slots + planes].reshape(rings, 2, planes, row_dev)

    whole_grad = landed_grad.transpose(4, 3, 2, 1, 0, 5).reshape(slots, -1, row_dev)
    whole_grad = jnp.pad(whole_grad, ((0, planes - slots), (0, 0), (0, 0)))
    whole_root = landed_root.transpose(2, 1, 0, 3).reshape(planes, 2 * rings, row_dev)
    slab = lax.axis_index("slab")
    own_cols = lax.dynamic_index_in_dim(owner_of.reshape(slabs, planes, 2), slab, 0, False)
    own_cols = lax.dynamic_index_in_dim(own_cols, half, 1, False)
    own_rank = lax.dynamic_index_in_dim(rank.reshape(slabs, planes, 2), slab, 0, False)
    own_rank = lax.dynamic_index_in_dim(own_rank, half, 1, False)
    landed_diag = landed[:, 2 * slots + planes]
    from_owner = own_cols[:, None] == half_turn(jnp.arange(owners))[None, :]
    whole_diag = sum(
        dot(
            (from_owner & (own_rank == at)[:, None]).astype(jnp.bfloat16),
            landed_diag[:, at * stripe : (at + 1) * stripe],
            ((1,), (0,)),
        )
        for at in range(2)
    )
    whole_diag = jnp.tile(whole_diag.astype(jnp.bfloat16), (1, row_dev // stripe))
    whole_diag = jnp.pad(whole_diag[:, None, :], ((0, 0), (0, 7), (0, 0)))
    grad_rows = whole_grad.shape[1]
    arrived = exchange(jnp.concatenate([whole_grad, whole_root, whole_diag], axis=1), T)
    own = (
        arrived[:, :grad_rows]
        .reshape(planes, 2, 2, tiles, rows, row_dev)
        .transpose(1, 2, 0, 4, 3, 5)
        .reshape(block, block)
    )
    inverse = 1.0 / block
    left_own = (dot(own, own, ((1,), (1,))) * inverse).astype(jnp.bfloat16)
    right_own = (dot(own, own, ((0,), (0,))) * inverse).astype(jnp.bfloat16)
    stats = jnp.stack(
        [left_own.reshape(planes, stripe, block), right_own.reshape(planes, stripe, block)], axis=1
    )
    own_root = arrived[:, grad_rows:]
    own_root, stats = lax.optimization_barrier((own_root, stats))
    stats = exchange(stats, T)[:slots].astype(jnp.float32)

    their_root = lax.ppermute(own_root, "core", [(0, 1), (1, 0)])
    ready = precondition(core, own_root, their_root, grad_block)
    keep = lax.dynamic_index_in_dim(ready, half, 0, keepdims=False)
    send = lax.dynamic_index_in_dim(ready, 1 - half, 0, keepdims=False)
    got = lax.ppermute(send, "half", [(0, 1), (1, 0)])
    first = jnp.where(half == 0, keep, got)
    second = jnp.where(half == 0, got, keep)
    return stats[:, 0], stats[:, 1], jnp.concatenate([first, second], axis=1)


def solution(mesh):
    owners, planes = mesh.devices.shape
    fine = Mesh(mesh.devices.reshape(owners // 4, 2, 2, planes), F + (T,))
    in_specs = (P(F, T), P(), P(F, None, None), P(F, T, None))
    out_specs = (P(F, T, None), P(F, T, None), P(F, T))
    return jax.shard_map(
        per_device, mesh=fine, in_specs=in_specs, out_specs=out_specs, check_vma=False
    )
```
